32 devices in a mesh: row: 4 (over y, core), col: 8 (over z, x).
Axes of the slice: x: 2, y: 2, z: 4, core: 2. Of those that a mesh axis runs over, the one named last changes fastest.
Arguments:
- band: float32 [8, 4, 4, 8, 512, 512], P(None, 'row', None, 'col'), as said below
Outputs:
- factored: float32 [8, 4, 4, 8, 512, 512], P(None, 'row', None, 'col')
Inputs may be any that keep to these rules, and one draw needn't show every extreme that they name: band holds the tiles of a symmetric matrix; its diagonal tiles are symmetric positive definite, and those of tile columns 0 and 1 leave every pivot of the steps positive.
All inputs are finite; a program needn't handle non-finite values.
Results may differ from the reference program's by a relative error of at most 0.00015.
Values sent between devices are 32-bit elements; how exact they have to be, the bound alone decides.
A program may use at most 192 MiB of HBM per device.

```python
import math
import jax
import jax.numpy as jnp
import numpy as np
from jax import lax

TILE = 512
BANDT = 32
STEPS = 2
GRID_ROWS = 4
GRID_COLS = 8
OPD = 8
CPD = 4


def draw_band(key, part):
    grid_rows = BANDT // OPD
    grid_cols = BANDT // CPD
    shape = (OPD, grid_rows, CPD, grid_cols, TILE, TILE)
    slot_idx = jnp.arange(OPD).reshape(-1, 1, 1, 1)
    row_idx = jnp.arange(grid_rows).reshape(1, -1, 1, 1)
    colgrp_idx = jnp.arange(CPD).reshape(1, 1, -1, 1)
    colpos_idx = jnp.arange(grid_cols).reshape(1, 1, 1, -1)
    column_of = colgrp_idx * grid_cols + colpos_idx
    offset_of = slot_idx * grid_rows + (row_idx - column_of) % grid_rows
    keys = jax.random.split(key, 4)
    diag_scale = 2.0 * math.sqrt(TILE)
    support_radius = 0.35
    root_three = math.sqrt(3.0)
    general = jax.random.uniform(keys[0], shape, jnp.float32, -root_three, root_three)
    linking = jax.random.uniform(keys[3], shape, jnp.float32, -0.2 * root_three, 0.2 * root_three)
    points = jax.random.uniform(keys[1], shape[:-2] + (3, TILE), jnp.float32, 0.0, 1.0)
    squared = jnp.zeros(shape, jnp.float32)
    for coord_index in range(3):
        coordinate = points[..., coord_index, :]
        difference = coordinate[..., :, None] - coordinate[..., None, :]
        squared = squared + difference * difference
    distance = jnp.sqrt(squared)
    kernel = jnp.square(jnp.maximum(1.0 - distance / support_radius, 0.0))
    nugget = jax.random.uniform(keys[2], shape[:-1], jnp.float32, 0.5, 1.0)
    eye_mask = jnp.arange(TILE)[:, None] == jnp.arange(TILE)[None, :]
    diag_tile = diag_scale * (kernel + jnp.where(eye_mask, nugget[..., :, None], 0.0))
    is_diag = (offset_of == 0)[..., None, None]
    is_link = ((column_of == 0) & (offset_of == 1))[..., None, None]
    return jnp.where(is_diag, diag_tile, jnp.where(is_link, linking, general))


def setup_inputs(seed: int = 0) -> dict:
    streams_of = jax.random.split(jax.random.key(seed), 2)
    return {
        "band": draw_band(jax.random.fold_in(streams_of[1], 71), 0),
    }


def reference(band):
    grid_rows = GRID_ROWS
    grid_cols = GRID_COLS
    highest = lax.Precision.HIGHEST
    columns = []
    for column_index in range(BANDT):
        offsets = np.arange(BANDT)
        columns.append(band[offsets // grid_rows, (column_index + offsets) % grid_rows, column_index // grid_cols, column_index % grid_cols])
    identity = jnp.eye(TILE, dtype=jnp.float32)
    for step in range(STEPS):
        factor = jnp.linalg.cholesky(columns[step][0])
        inverse = lax.linalg.triangular_solve(factor, identity, left_side=True, lower=True)
        panel = jnp.einsum('dab,cb->dac', columns[step], inverse, precision=highest)
        panel = panel.at[0].set(factor)
        columns[step] = panel
        for target in range(step + 1, BANDT):
            count = step + BANDT - target
            update = jnp.einsum('dab,cb->dac', panel[target - step:target - step + count], panel[target - step], precision=highest)
            columns[target] = columns[target].at[:count].add(-update)
    stacked = jnp.stack(columns)
    slot_idx, row_idx, colgrp_idx, colpos_idx = np.meshgrid(np.arange(OPD), np.arange(grid_rows), np.arange(CPD), np.arange(grid_cols), indexing='ij')
    column_of = colgrp_idx * grid_cols + colpos_idx
    offset_of = slot_idx * grid_rows + (row_idx - column_of) % grid_rows
    return stacked[column_of, offset_of]
```

```python
import functools

import jax
import jax.numpy as jnp
from jax import lax
from jax.experimental import pallas as pl
from jax.experimental.pallas import tpu as pltpu
from jax.sharding import PartitionSpec as P

STEPS = 2
BLOCK = 128
MESH = pl.DeviceIdType.MESH
NT = (((1,), (1,)), ((), ()))
NN = (((1,), (0,)), ((), ()))


def exact(a, b, dims):
    return lax.dot_general(a, b, dims, precision=lax.Precision.HIGHEST, preferred_element_type=jnp.float32)


def split(x):
    hi = x.astype(jnp.bfloat16)
    return hi, (x - hi.astype(jnp.float32)).astype(jnp.bfloat16)


def three(ah, al, bh, bl):
    dot = functools.partial(lax.dot_general, dimension_numbers=NT, preferred_element_type=jnp.float32)
    return dot(ah, bh) + (dot(ah, bl) + dot(al, bh))


def spread_kernel(band, rows, seeds, chain_send, chain_recv, peer_send, peer_recv, across_send, across_recv, across_own,
                  seed_send, seed_recv):
    n = lax.axis_size("row")
    grid_cols = lax.axis_size("col")
    slots, groups = band.shape[:2]
    r = lax.axis_index("row")
    c = lax.axis_index("col")
    lane = lax.rem(c, STEPS)
    other = 1 - lane
    peer = c + 1 - 2 * lane
    first = c < STEPS
    last = c >= grid_cols - STEPS
    before = jnp.where(first, c, c - STEPS)
    after = jnp.where(last, c, c + STEPS)
    place = lax.rem(r - lax.rem(c, n) + n, n)
    below = lax.rem(r + 1, n)

    barrier = pltpu.get_barrier_semaphore()

    @pl.when(jnp.logical_not(first))
    def _():
        pl.semaphore_signal(barrier, inc=1, device_id=(r, before), device_id_type=MESH)

    @pl.when(jnp.logical_not(last))
    def _():
        pl.semaphore_signal(barrier, inc=1, device_id=(r, after), device_id_type=MESH)

    pl.semaphore_signal(barrier, inc=1, device_id=(r, peer), device_id_type=MESH)
    for hop in range(1, n):
        pl.semaphore_signal(barrier, inc=1, device_id=(lax.rem(r + hop, n), c), device_id_type=MESH)
    pl.semaphore_wait(barrier, n + jnp.where(first, 0, 1) + jnp.where(last, 0, 1))

    @pl.when(first)
    def _():
        @pl.loop(0, slots)
        def _(s):
            pltpu.make_async_copy(band.at[s, 0], rows.at[lane, s], chain_recv.at[s]).start()

    def chain_copy(s):
        return pltpu.make_async_remote_copy(
            rows.at[lane, s], rows.at[lane, s], chain_send.at[s], chain_recv.at[s],
            device_id=(r, after), device_id_type=MESH)

    def peer_copy(s, which):
        return pltpu.make_async_remote_copy(
            rows.at[which, s], rows.at[which, s], peer_send.at[s], peer_recv.at[s],
            device_id=(r, peer), device_id_type=MESH)

    def across_copy(k, g, source):
        return pltpu.make_async_remote_copy(
            rows.at[k, source], rows.at[k, slots + g], across_send.at[k, g], across_recv.at[k, g],
            device_id=(below, c), device_id_type=MESH)

    def own_copy(k, g, source):
        return pltpu.make_async_copy(rows.at[k, source], rows.at[k, slots + g], across_own.at[k, g])

    def seed_copy(k, which, hop):
        return pltpu.make_async_remote_copy(
            rows.at[k, 0], seeds.at[which], seed_send.at[which, hop], seed_recv.at[which],
            device_id=(lax.rem(r + hop, n), c), device_id_type=MESH)

    def source_slot(k, g):
        return jnp.clip((g * grid_cols + c - k + n) // n - 1, 0, slots - 1)

    seed_list = ((0, 0, 0), (0, 1, 1), (1, 1, 2))

    def receive(s):
        chain_copy(s).wait_recv()

        @pl.when(jnp.logical_not(last))
        def _():
            chain_copy(s).start()

        peer_copy(s, lane).start()

    def pass_on(s):
        peer_copy(s, other).wait_recv()
        for k in range(STEPS):
            for g in range(groups):
                slot = source_slot(k, g)

                @pl.when(jnp.logical_and(place == 0, slot == s))
                def _():
                    across_copy(k, g, s).start()
                    own_copy(k, g, s).start()

    receive(0)
    pass_on(0)
    for k, root, which in seed_list:
        @pl.when(r == root)
        def _():
            for hop in range(1, n):
                seed_copy(k, which, hop).start()
            pltpu.make_async_copy(rows.at[k, 0], seeds.at[which], seed_recv.at[which]).start()

    receive(1)

    @pl.loop(2, slots)
    def _(s):
        receive(s)
        pass_on(s - 1)

    pass_on(slots - 1)

    for g in range(groups):
        for k in range(STEPS):
            @pl.when(place > 0)
            def _():
                across_copy(k, g, slots + g).wait_recv()

                @pl.when(place < n - 1)
                def _():
                    across_copy(k, g, slots + g).start()

    for k, root, which in seed_list:
        seed_copy(k, which, 1).wait_recv()

        @pl.when(r == root)
        def _():
            for hop in range(1, n):
                seed_copy(k, which, hop).wait_send()

    for g in range(groups):
        for k in range(STEPS):
            @pl.when(place == 0)
            def _():
                own_copy(k, g, 0).wait()

            @pl.when(place < n - 1)
            def _():
                across_copy(k, g, slots + g).wait_send()

    @pl.loop(0, slots)
    def _(s):
        peer_copy(s, lane).wait_send()

        @pl.when(jnp.logical_not(last))
        def _():
            chain_copy(s).wait_send()


def factor_block(block):
    size = block.shape[0]
    row_ids = lax.broadcasted_iota(jnp.int32, (size, size), 0)
    lane_ids = lax.broadcasted_iota(jnp.int32, (size, size), 1)
    eye = (row_ids == lane_ids).astype(jnp.float32)

    def eliminate(k, carry):
        left, right = carry
        column = jnp.sum(jnp.where(lane_ids == k, left, 0.0), axis=1, keepdims=True)
        here = row_ids == k
        row_left = jnp.sum(jnp.where(here, left, 0.0), axis=0, keepdims=True)
        row_right = jnp.sum(jnp.where(here, right, 0.0), axis=0, keepdims=True)
        pivot = jnp.sum(jnp.where(lane_ids[:1] == k, row_left, 0.0), axis=1, keepdims=True)
        column = jnp.where(row_ids[:, :1] > k, column, 0.0)
        scale = 1.0 / pivot
        return left - column * (row_left * scale), right - column * (row_right * scale)

    left, right = lax.fori_loop(0, size, eliminate, (block, eye))
    pivots = jnp.sum(jnp.where(row_ids == lane_ids, left, 0.0), axis=1, keepdims=True)
    scale = 1.0 / jnp.sqrt(pivots)
    upper = jnp.where(lane_ids >= row_ids, left * scale, 0.0)
    return upper.T, jnp.where(lane_ids <= row_ids, right * scale, 0.0)


def factor_tile(work, factor, inverse):
    size = work.shape[0]
    factor[...] = jnp.zeros_like(factor)
    inverse[...] = jnp.zeros_like(inverse)
    for start in range(0, size, BLOCK):
        end = start + BLOCK
        here = slice(start, end)
        lower, back = factor_block(work[here, here])
        factor[here, here] = lower
        inverse[here, here] = back
        if start:
            so_far = exact(factor[here, :start], inverse[:start, :start], NN)
            inverse[here, :start] = -exact(back, so_far, NN)
        if end < size:
            panel = exact(work[end:, here], back, NT)
            factor[end:, here] = panel
            work[end:, end:] = work[end:, end:] - exact(panel, panel, NT)


def factor_kernel(seeds, factors, inverses, link, work):
    work[...] = seeds[0]
    factor_tile(work, factors.at[0], inverses.at[0])
    link[...] = exact(seeds[1], inverses[0], NT)
    work[...] = seeds[2] - exact(link[...], link[...], NT)
    factor_tile(work, factors.at[1], inverses.at[1])


def panel_kernel(table, raw0, raw1, inverses, link, high, low, parts_high, parts_low):
    e = pl.program_id(0)
    tile = link.shape[0]

    @pl.when(e == 0)
    def _():
        for at, value in ((0, inverses[0]), (1, inverses[1]), (2, link[...])):
            hi, lo = split(value)
            parts_high[at] = hi
            parts_low[at] = lo

    first = three(*split(raw0[...]), parts_high[0], parts_low[0])
    first = jnp.where(table[1, e] > 0, first, 0.0)
    hi, lo = split(first)
    high[:, :tile] = hi
    low[:, :tile] = lo
    second = raw1[...] - three(hi, lo, parts_high[2], parts_low[2])
    hi, lo = split(three(*split(second), parts_high[1], parts_low[1]))
    high[:, tile:] = hi
    low[:, tile:] = lo


def update_kernel(table, local, high, low, factors, out):
    e = pl.program_id(0)
    mode = table[0, e]
    mine = table[1, e]
    across = table[2, e]
    step = table[3, e]
    tile = local.shape[0]

    @pl.when(mode == 0)
    def _():
        out[...] = local[...]

    @pl.when(mode == 1)
    def _():
        out[...] = local[...] - three(high[mine], low[mine], high[across], low[across])

    for k in range(STEPS):
        @pl.when(jnp.logical_and(mode == 2, step == k))
        def _():
            cut = slice(k * tile, (k + 1) * tile)
            out[...] = high[mine, :, cut].astype(jnp.float32) + low[mine, :, cut].astype(jnp.float32)

    @pl.when(mode == 3)
    def _():
        out[...] = factors[step]


def shards(band):
    slots, _, groups, _, tile, _ = band.shape
    n = lax.axis_size("row")
    grid_cols = lax.axis_size("col")
    bandt = slots * n
    r = lax.axis_index("row")
    c = lax.axis_index("col")
    f32 = jnp.float32
    local = band.reshape(slots, groups, tile, tile)
    dma = pltpu.SemaphoreType.DMA
    anywhere = pl.BlockSpec(memory_space=pl.ANY)
    in_vmem = pl.BlockSpec(memory_space=pltpu.VMEM)
    entries = slots + groups
    limit = 56 * 1024 * 1024

    rows, seeds = pl.pallas_call(
        spread_kernel,
        out_shape=(jax.ShapeDtypeStruct((STEPS, entries, tile, tile), f32), jax.ShapeDtypeStruct((3, tile, tile), f32)),
        in_specs=[anywhere],
        out_specs=(anywhere, anywhere),
        scratch_shapes=[dma((slots,)), dma((slots,)), dma((slots,)), dma((slots,)), dma((STEPS, groups)),
                        dma((STEPS, groups)), dma((STEPS, groups)), dma((3, n)), dma((3,))],
        compiler_params=pltpu.CompilerParams(collective_id=0, has_side_effects=True),
        name="spread_columns",
    )(local)

    square = jax.ShapeDtypeStruct((STEPS, tile, tile), f32)
    factors, inverses, link = pl.pallas_call(
        factor_kernel,
        out_shape=(square, square, jax.ShapeDtypeStruct((tile, tile), f32)),
        in_specs=[in_vmem],
        out_specs=(in_vmem, in_vmem, in_vmem),
        scratch_shapes=[pltpu.VMEM((tile, tile), f32)],
        compiler_params=pltpu.CompilerParams(vmem_limit_bytes=limit),
        name="factor_diagonals",
    )(seeds)

    entry = jnp.arange(entries, dtype=jnp.int32)
    group_of = jnp.maximum(entry - slots, 0)
    row_of = jnp.where(entry < slots, 1 + entry * n + (r - 1) % n, group_of * grid_cols + c)
    source = jnp.where(entry < slots, jnp.minimum(row_of // n, slots - 1), entry)
    table = jnp.stack([source, (row_of < bandt).astype(jnp.int32)])
    half = jax.ShapeDtypeStruct((entries, tile, STEPS * tile), jnp.bfloat16)
    once = pl.Buffered(1)
    high, low = pl.pallas_call(
        panel_kernel,
        out_shape=(half, half),
        grid_spec=pltpu.PrefetchScalarGridSpec(
            num_scalar_prefetch=1,
            grid=(entries,),
            in_specs=[
                pl.BlockSpec((None, None, tile, tile), lambda e, t: (0, t[0, e], 0, 0)),
                pl.BlockSpec((None, None, tile, tile), lambda e, t: (1, e, 0, 0)),
                pl.BlockSpec((STEPS, tile, tile), lambda e, t: (0, 0, 0), pipeline_mode=once),
                pl.BlockSpec((tile, tile), lambda e, t: (0, 0), pipeline_mode=once),
            ],
            out_specs=[pl.BlockSpec((None, tile, STEPS * tile), lambda e, t: (e, 0, 0))] * 2,
            scratch_shapes=[pltpu.VMEM((3, tile, tile), jnp.bfloat16)] * 2,
        ),
        compiler_params=pltpu.CompilerParams(vmem_limit_bytes=limit),
        name="panels",
    )(table, rows, rows, inverses, link)

    count = slots * groups
    at = jnp.arange(count, dtype=jnp.int32)
    slot = at // groups
    group = at % groups
    column = group * grid_cols + c
    row = column + slot * n + (r - column) % n
    mode = jnp.where(column < STEPS, jnp.where(row == column, 3, 2), jnp.where(row <= bandt, 1, 0))
    step = jnp.minimum(column, STEPS - 1)
    mine = jnp.clip((row + n - 1) // n - 1, 0, slots - 1)
    table = jnp.stack([mode, mine, slots + group, step]).astype(jnp.int32)
    whole = pl.BlockSpec((entries, tile, STEPS * tile), lambda e, t: (0, 0, 0), pipeline_mode=once)
    block = pl.BlockSpec((None, None, tile, tile), lambda e, t: (e // groups, e % groups, 0, 0))
    out = pl.pallas_call(
        update_kernel,
        out_shape=jax.ShapeDtypeStruct(local.shape, f32),
        grid_spec=pltpu.PrefetchScalarGridSpec(
            num_scalar_prefetch=1,
            grid=(count,),
            in_specs=[block, whole, whole,
                      pl.BlockSpec((STEPS, tile, tile), lambda e, t: (0, 0, 0), pipeline_mode=once)],
            out_specs=block,
        ),
        compiler_params=pltpu.CompilerParams(vmem_limit_bytes=limit),
        name="updates",
    )(table, local, high, low, factors)
    return out.reshape(slots, 1, groups, 1, tile, tile)


def solution(mesh):
    return jax.shard_map(
        shards,
        mesh=mesh,
        in_specs=(P(None, "row", None, "col", None, None),),
        out_specs=P(None, "row", None, "col", None, None),
        check_vma=False,
    )
```
